512 devices in a mesh: role: 8 (over x_hi, y), dp: 64 (over z, x_lo, core).
Axes of the slice: x: 4 (x_hi: 2, x_lo: 2; x = x_hi * 2 + x_lo), y: 4, z: 16, core: 2. Of those that a mesh axis runs over, the one named last changes fastest.
Arguments:
- inputs: bfloat16 [16384, 6144], P('dp'), may hold values from -16 to 16
- cotangent: bfloat16 [16384, 1024], P('dp', 'role'), may hold values from -0.046875 to 0.046875
- owner: int32 [24], replicated, may hold values from 0 to 63, as said below
- step: int32 [1], replicated, may hold values from 16 to 127
Outputs:
- update: bfloat16 [6144, 1024], P('dp', 'role')
- roots: bfloat16 [64, 2, 2, 512, 512], P('dp', None, None, 'role')
The draws below stay inside these ranges and needn't reach their ends.
Inputs may be any that keep to these rules, and one draw needn't show every extreme that they name: `owner`: no index owns more than 2 blocks, and at least one owns exactly 2.
All inputs are finite; a program needn't handle non-finite values.
Results may differ from the reference program's by a relative error of at most 0.012.
The reference program's roundings to bfloat16 on the way count: a program that leaves them out, or rounds other values in their place, can miss the bound.
Values may be sent and summed in bfloat16 or wider, within the bound.
No kernel may reach another device: no remote copies, remote signals or barrier semaphores. Data moves between devices by JAX's collectives and lax.ppermute only.
A program may use at most 64 MiB of HBM per device.

```python
import jax
import jax.numpy as jnp
from jax import lax

D = 6144
B = 512
SLOTS = 2
NEWTON = 2
TOKENS = 16384
FW = 1024
NBLK = 24
N_DP = 64


def draw_owner(key, part):
    key = jax.random.fold_in(key, 7)
    first, second, third = jax.random.split(key, 3)
    full = jax.random.randint(first, (), 0, N_DP).astype(jnp.int32)
    others = (jax.random.permutation(second, (N_DP - 1) * SLOTS)[:NBLK - SLOTS] // SLOTS).astype(jnp.int32)
    others = others + (others >= full).astype(jnp.int32)
    table = jnp.concatenate([jnp.zeros((SLOTS,), jnp.int32) + full, others])
    return jax.random.permutation(third, table).astype(jnp.int32)


def with_spikes(array, stream_key, source, target, blocks, factor):
    def block_of(dim):
        return (jnp.arange(array.shape[dim]) // (array.shape[dim] // blocks)).reshape((-1,) + (1,) * (array.ndim - 1 - dim))

    near = jax.random.permutation(stream_key, blocks)[block_of(target)]
    second = (block_of(target) + blocks // 2) % blocks
    return jnp.where((block_of(source) == near) | (block_of(source) == second), factor * array, array)


def shard_levels(own_key, dims, shards, low, largest):
    def one(dim, shards_of):
        steps = jax.random.uniform(jax.random.fold_in(jax.random.fold_in(own_key, 6), dim), (shards_of,), jnp.float32, low / len(shards), largest / len(shards))
        return jnp.repeat(jnp.exp(steps), dims[dim] // shards_of).reshape((-1,) + (1,) * (len(dims) - dim - 1))

    factor_of = one(*shards[0])
    for cut in shards[1:]:
        factor_of = factor_of * one(*cut)
    return factor_of


def scatter_about(key, dims, deviation, bound, pieces=(), held_as=jnp.bfloat16):
    array = jax.random.normal(key, dims, jnp.float32) * deviation
    if len(pieces) > 0:
        array = shard_levels(key, dims, pieces, -0.22, 0.18) * array
    return jnp.clip(array, min=-bound, max=bound).astype(held_as)


def heavy_noise(stream_key, extent, width, most, cuts, heavy, held_as=jnp.bfloat16):
    values = width * jax.random.normal(stream_key, extent, jnp.float32)
    if cuts:
        values = values * shard_levels(stream_key, extent, cuts, -0.22, 0.18)
    return jnp.clip(with_spikes(values, jax.random.fold_in(stream_key, 3), *heavy), -most, most).astype(held_as)


def setup_inputs(seed: int = 0) -> dict:
    seeds = jax.random.split(jax.random.key(seed), 5)
    return {
        "inputs": heavy_noise(seeds[0], (TOKENS, D), 1.0, 16.0, ((0, 64),), (0, 1, 64, 4.0)),
        "cotangent": scatter_about(seeds[1], (TOKENS, FW), (TOKENS ** -0.5), 0.046875, ((0, 64), (1, 8))),
        "owner": draw_owner(jax.random.fold_in(seeds[4], 71), 0),
        "step": jax.random.randint(seeds[3], (1,), 16, 128).astype(jnp.int32),
    }


peak_rate = 20.0
warm_steps = 64.0

def batched(left, right):
    return jnp.einsum('kij,kjl->kil', left.astype(jnp.float32), right.astype(jnp.float32))

def inverse_root(stats):
    eye = jnp.eye(stats.shape[-1], dtype=jnp.float32)
    norm = jnp.sqrt(lax.optimization_barrier(jnp.sum(stats * stats, axis=(1, 2), keepdims=True)) + 1e-06)
    scale = 2.5 / norm
    current = scale * stats
    root = None
    for turn in range(NEWTON):
        factor = ((5.0 * eye - current) * 0.25).astype(jnp.bfloat16)
        if turn == 0:
            root = (jnp.sqrt(jnp.sqrt(scale)) * factor.astype(jnp.float32)).astype(jnp.bfloat16)
        else:
            root = batched(root, factor).astype(jnp.bfloat16)
        if turn + 1 < NEWTON:
            square = batched(factor, factor).astype(jnp.bfloat16)
            fourth = batched(square, square).astype(jnp.bfloat16)
            current = batched(fourth, current.astype(jnp.bfloat16))
    return root

def one_block(block):
    left = jnp.dot(block, block.T, preferred_element_type=jnp.float32)
    right = jnp.dot(block.T, block, preferred_element_type=jnp.float32)
    roots = inverse_root(jnp.stack([left, right]))
    mixed = jnp.dot(block, roots[1], preferred_element_type=jnp.float32).astype(jnp.bfloat16)
    update = jnp.dot(roots[0], mixed, preferred_element_type=jnp.float32).astype(jnp.bfloat16)
    return (roots, update)

def reference(inputs, cotangent, owner, step):
    grad = jnp.dot(inputs.T, cotangent, preferred_element_type=jnp.float32)
    rows = D // B
    cols = FW // B
    blocks = grad.astype(jnp.bfloat16).reshape(rows, B, cols, B).transpose(0, 2, 1, 3).reshape(rows * cols, B, B)
    roots, update = lax.map(one_block, blocks)
    rate = peak_rate * jnp.minimum(1.0, (step[0].astype(jnp.float32) + 1.0) / warm_steps)
    whole = update.reshape(rows, cols, B, B).transpose(0, 2, 1, 3).reshape(D, FW).astype(jnp.float32)
    new_update = (-rate * whole).astype(jnp.bfloat16)
    owners = jnp.arange(N_DP, dtype=jnp.int32)
    mine = (owner[None, :] == owners[:, None]).astype(jnp.int32)
    rank = jnp.cumsum(mine, axis=1) - 1
    hits = mine[:, None, :] * (rank[:, None, :] == jnp.arange(SLOTS, dtype=jnp.int32)[None, :, None]).astype(jnp.int32)
    slot_block = lax.optimization_barrier(jnp.sum(hits * jnp.arange(NBLK, dtype=jnp.int32)[None, None, :], axis=2)).astype(jnp.int32)
    valid = lax.optimization_barrier(jnp.sum(hits, axis=2))
    slot_roots = roots[slot_block] * valid[:, :, None, None, None].astype(jnp.bfloat16)
    return (new_update, slot_roots)
```

```python
import functools

import jax
import jax.numpy as jnp
from jax import lax
from jax.experimental import pallas as pl
from jax.experimental.pallas import tpu as pltpu
from jax.sharding import Mesh, PartitionSpec as P

B = 512
peak_rate = 20.0
warm_steps = 64.0
bf16 = jnp.bfloat16
f32 = jnp.float32

NZ, NY = 16, 4
NBLK, BROWS = 24, 12
PIECE = B // NZ
LANE_BLOCKS = 3
WIN = 128

NT = (((1,), (1,)), ((), ()))
TN = (((0,), (0,)), ((), ()))


def all_to_all(value, axis):
    return lax.all_to_all(value, axis, 0, 0, tiled=True)


def pack_kernel(owner_ref, place_ref, pieces_ref, out_ref, count_ref):
    lane, xh = place_ref[0], place_ref[1]
    for z in range(NZ):
        count_ref[z] = 0
        out_ref[z, :PIECE, :] = jnp.zeros((PIECE, 128), bf16)
        index = z * 4 + lane
        turn = index % 16
        row = 3 * (index // 16) + (turn >= 5).astype(jnp.int32) + (turn >= 11).astype(jnp.int32)
        out_ref[z, PIECE:, :] = pieces_ref[xh * BROWS + row]

    for b in range(NBLK):
        who = owner_ref[b]
        z = who // 4
        mine = who % 4 == lane
        rank = count_ref[z]

        @pl.when(mine)
        def _():
            count_ref[z] = rank + 1

            @pl.when(rank == xh)
            def _():
                out_ref[z, :PIECE, :] = pieces_ref[(b % 2) * BROWS + b // 2]


def pack(owner, place, pieces):
    return pl.pallas_call(
        pack_kernel,
        out_shape=jax.ShapeDtypeStruct((NZ, 2 * PIECE, 128), bf16),
        in_specs=[
            pl.BlockSpec(memory_space=pltpu.SMEM),
            pl.BlockSpec(memory_space=pltpu.SMEM),
            pl.BlockSpec(memory_space=pltpu.VMEM),
        ],
        out_specs=pl.BlockSpec(memory_space=pltpu.VMEM),
        scratch_shapes=[pltpu.SMEM((NZ,), jnp.int32)],
        name="pack",
    )(owner, place, pieces)


def root_rows(stat, parts, x_ref, c_ref):
    scale = 2.5 * lax.rsqrt(jnp.sum(stat * stat, keepdims=True) + 1e-06)
    current = scale * stat
    row = lax.broadcasted_iota(jnp.int32, (B, B), 0)
    col = lax.broadcasted_iota(jnp.int32, (B, B), 1)
    factor = (jnp.where(row == col, 1.25, 0.0) - 0.25 * current).astype(bf16)
    x_ref[...] = factor
    c_ref[...] = current.astype(bf16)
    root = (jnp.sqrt(jnp.sqrt(scale)) * factor.astype(f32)).astype(bf16)

    def dot(left, right):
        return jnp.dot(left, right, preferred_element_type=f32)

    rows = jnp.concatenate([x_ref[pl.ds(start, size), :] for start, size in parts], axis=0)
    eye = jnp.concatenate(
        [
            jnp.where(
                lax.broadcasted_iota(jnp.int32, (size, B), 0) + start
                == lax.broadcasted_iota(jnp.int32, (size, B), 1),
                1.25,
                0.0,
            )
            for start, size in parts
        ],
        axis=0,
    )
    square = dot(rows, factor).astype(bf16)
    fourth = dot(dot(square, factor).astype(bf16), factor).astype(bf16)
    second = (eye - 0.25 * dot(fourth, c_ref[...])).astype(bf16)
    return dot(second, root).astype(bf16)


def block_of(got_ref, which):
    return jnp.concatenate([got_ref[y, which] for y in range(NY)], axis=1)


def owned_kernel(place_ref, got_ref, out_ref, xl_ref, cl_ref, xr_ref, cr_ref):
    y, valid = place_ref[2], place_ref[3]
    block = block_of(got_ref, 0)
    left = lax.dot_general(block, block, NT, preferred_element_type=f32)
    right = lax.dot_general(block, block, TN, preferred_element_type=f32)
    share = B // 8
    first = pl.multiple_of(y * share, share)
    second = pl.multiple_of(y * share + B // 2, share)
    parts = ((first, share), (second, share))
    keep = valid.astype(f32)
    for side, (stat, x_ref, c_ref) in enumerate(((left, xl_ref, cl_ref), (right, xr_ref, cr_ref))):
        rows = (root_rows(stat, parts, x_ref, c_ref).astype(f32) * keep).astype(bf16)
        out_ref[0, side] = rows[:share]
        out_ref[1, side] = rows[share:]


def home_kernel(place_ref, got_ref, out_ref, xl_ref, cl_ref, xr_ref, cr_ref):
    y, start = place_ref[2], place_ref[4]
    block = block_of(got_ref, 1)
    left = lax.dot_general(block, block, NT, preferred_element_type=f32)
    right = lax.dot_general(block, block, TN, preferred_element_type=f32)
    hr = root_rows(right, ((pl.multiple_of(y * 128, 128), 128),), xr_ref, cr_ref)
    hl = root_rows(left, ((pl.multiple_of(start, 32), WIN),), xl_ref, cl_ref)
    mixed = lax.dot_general(block, hr, NT, preferred_element_type=f32).astype(bf16)
    out_ref[...] = jnp.dot(hl, mixed, preferred_element_type=f32).astype(bf16)


def block_call(kernel, out_shape, place, got, name):
    return pl.pallas_call(
        kernel,
        out_shape=jax.ShapeDtypeStruct(out_shape, bf16),
        in_specs=[
            pl.BlockSpec(memory_space=pltpu.SMEM),
            pl.BlockSpec(memory_space=pltpu.VMEM),
        ],
        out_specs=pl.BlockSpec(memory_space=pltpu.VMEM),
        scratch_shapes=[pltpu.VMEM((B, B), bf16)] * 4,
        compiler_params=pltpu.CompilerParams(vmem_limit_bytes=32 * 1024 * 1024),
        name=name,
    )(place, got)


def per_device(inputs, cotangent, owner, step):
    xh, y, z = lax.axis_index("xh"), lax.axis_index("y"), lax.axis_index("z")
    xl, c = lax.axis_index("xl"), lax.axis_index("c")
    lane = xl * 2 + c
    index = z * 4 + lane

    grad = lax.dot_general(inputs, cotangent, TN, preferred_element_type=f32).astype(bf16)
    got = all_to_all(grad.reshape(2, -1, 128), "c")
    grad = (got[0].astype(f32) + got[1].astype(f32)).astype(bf16)
    got = all_to_all(grad.reshape(2, -1, 128), "xl")
    grad = (got[0].astype(f32) + got[1].astype(f32)).astype(bf16)
    grad = grad.reshape(LANE_BLOCKS, NZ, PIECE, 128).transpose(1, 0, 2, 3)
    got = all_to_all(grad, "z")
    piece = jnp.sum(got.astype(f32), axis=0).astype(bf16)

    lanes = lax.all_gather(piece, ("c", "xl"))
    pieces = lax.all_gather(lanes, "xh").reshape(NBLK, PIECE, 128)

    turn = index % 16
    first = jnp.where(turn < 5, 96 * turn, jnp.where(turn < 11, 96 * turn - 512, 96 * turn - 1024))
    start = jnp.where(turn == 11, 0, jnp.clip(first, 0, B - WIN))
    valid = jnp.sum((owner == index).astype(jnp.int32)) > xh
    place = jnp.stack([lane, xh, y, valid.astype(jnp.int32), start]).astype(jnp.int32)

    sent = pack(owner, place, pieces)
    got = all_to_all(sent, "z")
    both = got.reshape(NZ, 2, PIECE, 128).transpose(1, 0, 2, 3).reshape(2, B, 128)
    got = all_to_all(jnp.broadcast_to(both[None], (NY, 2, B, 128)), "y")

    share = B // 8
    rows = block_call(owned_kernel, (2, 2, share, B), place, got, "owned")
    keep = lax.dynamic_index_in_dim(rows, xh, 0, False)
    give = lax.dynamic_index_in_dim(rows, 1 - xh, 0, False)
    swap = [(0, 1), (1, 0)]
    received = lax.ppermute(give, "xh", swap)
    window = block_call(home_kernel, (WIN, 128), place, got, "home")
    spare = jnp.where(turn == 4, window[WIN - 32 :], window[:32])
    extra = lax.ppermute(spare, "c", swap)
    roots = jnp.where(xh == 0, jnp.stack([keep, received]), jnp.stack([received, keep]))[None]

    whole = jnp.concatenate([extra, window, extra], axis=0)
    offset = jnp.where(turn == 5, 0, jnp.where(turn == 10, 96, 32 + first - start))
    mine = lax.dynamic_slice_in_dim(whole, offset, 96, 0)
    rate = peak_rate * jnp.minimum(1.0, (step[0].astype(f32) + 1.0) / warm_steps)
    update = (-rate * mine.astype(f32)).astype(bf16)
    return (update, roots)


def solution(mesh):
    split = Mesh(mesh.devices.reshape(2, NY, NZ, 2, 2), ("xh", "y", "z", "xl", "c"))
    return jax.shard_map(
        per_device,
        mesh=split,
        in_specs=(
            P(("z", "xl", "c"), None),
            P(("z", "xl", "c"), ("xh", "y")),
            P(),
            P(),
        ),
        out_specs=(
            P(("z", "xl", "c"), ("xh", "y")),
            P(("z", "xl", "c"), None, None, ("xh", "y"), None),
        ),
        check_vma=False,
    )
```

```python
import functools

import jax
import jax.numpy as jnp
from jax import lax
from jax.experimental import pallas as pl
from jax.experimental.pallas import tpu as pltpu
from jax.sharding import Mesh, PartitionSpec as P

B = 512
peak_rate = 20.0
warm_steps = 64.0
bf16 = jnp.bfloat16
f32 = jnp.float32

NZ, NY = 16, 4
NBLK, BROWS = 24, 12
PIECE = B // NZ
LANE_BLOCKS = 3
WIN = 128

NT = (((1,), (1,)), ((), ()))
TN = (((0,), (0,)), ((), ()))


def all_to_all(value, axis):
    return lax.all_to_all(value, axis, 0, 0, tiled=True)


def partial_kernel(place_ref, inputs_ref, cotangent_ref, out_ref):
    out_ref[...] = lax.dot_general(
        inputs_ref[...], cotangent_ref[...], TN, preferred_element_type=f32
    ).astype(bf16)


def partial_grad(half, inputs, cotangent, name):
    tokens, width = inputs.shape
    steps, tile = 3, width // 6
    return pl.pallas_call(
        partial_kernel,
        out_shape=jax.ShapeDtypeStruct((width // 2, 128), bf16),
        grid_spec=pltpu.PrefetchScalarGridSpec(
            num_scalar_prefetch=1,
            grid=(steps,),
            in_specs=[
                pl.BlockSpec((tokens, tile), lambda i, half: (0, half[0] * steps + i)),
                pl.BlockSpec((tokens, 128), lambda i, half: (0, 0)),
            ],
            out_specs=pl.BlockSpec((tile, 128), lambda i, half: (i, 0)),
        ),
        name=name,
    )(half, inputs, cotangent)


def fold_kernel(got_ref, out_ref):
    for k in range(LANE_BLOCKS):
        for z in range(NZ):
            rows = pl.ds((k * NZ + z) * PIECE, PIECE)
            total = got_ref[0, rows, :].astype(f32) + got_ref[1, rows, :].astype(f32)
            out_ref[z, pl.ds(k * PIECE, PIECE), :] = total.astype(bf16)


def fold(got):
    return pl.pallas_call(
        fold_kernel,
        out_shape=jax.ShapeDtypeStruct((NZ, LANE_BLOCKS * PIECE, 128), bf16),
        in_specs=[pl.BlockSpec(memory_space=pltpu.VMEM)],
        out_specs=pl.BlockSpec(memory_space=pltpu.VMEM),
        name="fold",
    )(got)


def total_kernel(got_ref, out_ref):
    total = got_ref[0].astype(f32)
    for z in range(1, NZ):
        total = total + got_ref[z].astype(f32)
    total = total.astype(bf16)
    for to in range(8):
        out_ref[to] = total


def total_of(got):
    return pl.pallas_call(
        total_kernel,
        out_shape=jax.ShapeDtypeStruct((8,) + got.shape[1:], bf16),
        in_specs=[pl.BlockSpec(memory_space=pltpu.VMEM)],
        out_specs=pl.BlockSpec(memory_space=pltpu.VMEM),
        name="total",
    )(got)


def pack_kernel(owner_ref, place_ref, pieces_ref, out_ref, count_ref):
    lane, xh = place_ref[0], place_ref[1]
    for z in range(NZ):
        count_ref[z] = 0
        out_ref[z, :PIECE, :] = jnp.zeros((PIECE, 128), bf16)
        index = z * 4 + lane
        turn = index % 16
        row = 3 * (index // 16) + (turn >= 5).astype(jnp.int32) + (turn >= 11).astype(jnp.int32)
        out_ref[z, PIECE:, :] = pieces_ref[xh * BROWS + row]

    for b in range(NBLK):
        who = owner_ref[b]
        z = who // 4
        mine = who % 4 == lane
        rank = count_ref[z]

        @pl.when(mine)
        def _():
            count_ref[z] = rank + 1

            @pl.when(rank == xh)
            def _():
                out_ref[z, :PIECE, :] = pieces_ref[(b % 2) * BROWS + b // 2]


def pack(owner, place, pieces):
    return pl.pallas_call(
        pack_kernel,
        out_shape=jax.ShapeDtypeStruct((NZ, 2 * PIECE, 128), bf16),
        in_specs=[
            pl.BlockSpec(memory_space=pltpu.SMEM),
            pl.BlockSpec(memory_space=pltpu.SMEM),
            pl.BlockSpec(memory_space=pltpu.VMEM),
        ],
        out_specs=pl.BlockSpec(memory_space=pltpu.VMEM),
        scratch_shapes=[pltpu.SMEM((NZ,), jnp.int32)],
        name="pack",
    )(owner, place, pieces)


def root_rows(stat, parts, x_ref, c_ref):
    scale = 2.5 * lax.rsqrt(jnp.sum(stat * stat, keepdims=True) + 1e-06)
    current = scale * stat
    row = lax.broadcasted_iota(jnp.int32, (B, B), 0)
    col = lax.broadcasted_iota(jnp.int32, (B, B), 1)
    factor = (jnp.where(row == col, 1.25, 0.0) - 0.25 * current).astype(bf16)
    x_ref[...] = factor
    c_ref[...] = current.astype(bf16)
    root = (jnp.sqrt(jnp.sqrt(scale)) * factor.astype(f32)).astype(bf16)

    def dot(left, right):
        return jnp.dot(left, right, preferred_element_type=f32)

    rows = jnp.concatenate([x_ref[pl.ds(start, size), :] for start, size in parts], axis=0)
    eye = jnp.concatenate(
        [
            jnp.where(
                lax.broadcasted_iota(jnp.int32, (size, B), 0) + start
                == lax.broadcasted_iota(jnp.int32, (size, B), 1),
                1.25,
                0.0,
            )
            for start, size in parts
        ],
        axis=0,
    )
    square = dot(rows, factor).astype(bf16)
    fourth = dot(dot(square, factor).astype(bf16), factor).astype(bf16)
    second = (eye - 0.25 * dot(fourth, c_ref[...])).astype(bf16)
    return dot(second, root).astype(bf16)


def block_of(got_ref, which):
    return jnp.concatenate([got_ref[y, which] for y in range(NY)], axis=1)


def owned_kernel(place_ref, got_ref, keep_ref, give_ref, xl_ref, cl_ref, xr_ref, cr_ref):
    xh, y, valid = place_ref[1], place_ref[2], place_ref[3]
    block = block_of(got_ref, 0)
    left = lax.dot_general(block, block, NT, preferred_element_type=f32)
    right = lax.dot_general(block, block, TN, preferred_element_type=f32)
    share = B // 8
    first = pl.multiple_of(y * share + xh * (B // 2), share)
    second = pl.multiple_of(y * share + (1 - xh) * (B // 2), share)
    parts = ((first, share), (second, share))
    keep = valid.astype(f32)
    for side, (stat, x_ref, c_ref) in enumerate(((left, xl_ref, cl_ref), (right, xr_ref, cr_ref))):
        rows = (root_rows(stat, parts, x_ref, c_ref).astype(f32) * keep).astype(bf16)
        keep_ref[side] = rows[:share]
        give_ref[side] = rows[share:]


def home_kernel(place_ref, got_ref, out_ref, xl_ref, cl_ref, xr_ref, cr_ref):
    y, start = place_ref[2], place_ref[4]
    block = block_of(got_ref, 1)
    left = lax.dot_general(block, block, NT, preferred_element_type=f32)
    right = lax.dot_general(block, block, TN, preferred_element_type=f32)
    hr = root_rows(right, ((pl.multiple_of(y * 128, 128), 128),), xr_ref, cr_ref)
    hl = root_rows(left, ((pl.multiple_of(start, 32), WIN),), xl_ref, cl_ref)
    mixed = lax.dot_general(block, hr, NT, preferred_element_type=f32).astype(bf16)
    out_ref[...] = jnp.dot(hl, mixed, preferred_element_type=f32).astype(bf16)


def block_call(kernel, out_shapes, place, got, name):
    return pl.pallas_call(
        kernel,
        out_shape=[jax.ShapeDtypeStruct(shape, bf16) for shape in out_shapes],
        in_specs=[
            pl.BlockSpec(memory_space=pltpu.SMEM),
            pl.BlockSpec(memory_space=pltpu.VMEM),
        ],
        out_specs=[pl.BlockSpec(memory_space=pltpu.VMEM)] * len(out_shapes),
        scratch_shapes=[pltpu.VMEM((B, B), bf16)] * 4,
        compiler_params=pltpu.CompilerParams(vmem_limit_bytes=32 * 1024 * 1024),
        name=name,
    )(place, got)


def per_device(inputs, cotangent, owner, step):
    xh, y, z = lax.axis_index("xh"), lax.axis_index("y"), lax.axis_index("z")
    xl, c = lax.axis_index("xl"), lax.axis_index("c")
    lane = xl * 2 + c
    index = z * 4 + lane

    swap = [(0, 1), (1, 0)]
    halves = lax.broadcasted_iota(jnp.int32, (1,), 0) + c
    inputs = pltpu.with_memory_space_constraint(inputs, pltpu.HBM)
    theirs = partial_grad(1 - halves, inputs, cotangent, "theirs")
    theirs = lax.ppermute(theirs, "c", swap)
    grad = partial_grad(halves, inputs, cotangent, "ours")
    grad = (grad.astype(f32) + theirs.astype(f32)).astype(bf16)
    got = all_to_all(grad.reshape(2, -1, 128), "xl")
    got = all_to_all(fold(got), "z")
    pieces = all_to_all(total_of(got), ("xh", "c", "xl")).reshape(NBLK, PIECE, 128)

    turn = index % 16
    first = jnp.where(turn < 5, 96 * turn, jnp.where(turn < 11, 96 * turn - 512, 96 * turn - 1024))
    start = jnp.where(turn == 11, 0, jnp.clip(first, 0, B - WIN))
    valid = jnp.sum((owner == index).astype(jnp.int32)) > xh
    place = jnp.stack([lane, xh, y, valid.astype(jnp.int32), start]).astype(jnp.int32)

    sent = pack(owner, place, pieces)
    got = all_to_all(sent, "z")
    both = got.reshape(NZ, 2, PIECE, 128).transpose(1, 0, 2, 3).reshape(2, B, 128)
    got = all_to_all(jnp.broadcast_to(both[None], (NY, 2, B, 128)), "y")

    share = B // 8
    half = (2, share, B)
    keep, give = block_call(owned_kernel, (half, half), place, got, "owned")
    received = lax.ppermute(give, "xh", swap)
    (window,) = block_call(home_kernel, ((WIN, 128),), place, got, "home")
    spare = jnp.where(turn == 4, window[WIN - 32 :], window[:32])
    extra = lax.ppermute(spare, "c", swap)
    roots = jnp.where(xh == 0, jnp.stack([keep, received]), jnp.stack([received, keep]))[None]

    whole = jnp.concatenate([extra, window, extra], axis=0)
    offset = jnp.where(turn == 5, 0, jnp.where(turn == 10, 96, 32 + first - start))
    mine = lax.dynamic_slice_in_dim(whole, offset, 96, 0)
    rate = peak_rate * jnp.minimum(1.0, (step[0].astype(f32) + 1.0) / warm_steps)
    update = (-rate * mine.astype(f32)).astype(bf16)
    return (update, roots)


def solution(mesh):
    split = Mesh(mesh.devices.reshape(2, NY, NZ, 2, 2), ("xh", "y", "z", "xl", "c"))
    return jax.shard_map(
        per_device,
        mesh=split,
        in_specs=(
            P(("z", "xl", "c"), None),
            P(("z", "xl", "c"), ("xh", "y")),
            P(),
            P(),
        ),
        out_specs=(
            P(("z", "xl", "c"), ("xh", "y")),
            P(("z", "xl", "c"), None, None, ("xh", "y"), None),
        ),
        check_vma=False,
    )
```

```python
import jax
import jax.numpy as jnp
from jax import lax
from jax.experimental import pallas as pl
from jax.experimental.pallas import tpu as pltpu
from jax.sharding import Mesh, PartitionSpec as P

B = 512
peak_rate = 20.0
warm_steps = 64.0
bf16 = jnp.bfloat16
f32 = jnp.float32

NZ, NY = 16, 4
NBLK, BROWS = 24, 12
PIECE = B // NZ
LANE_BLOCKS = 3
WIN = 128

NT = (((1,), (1,)), ((), ()))
TN = (((0,), (0,)), ((), ()))


def all_to_all(value, axis):
    return lax.all_to_all(value, axis, 0, 0, tiled=True)


def where_am_i():
    z = ((lax.axis_index("za") * 2 + lax.axis_index("zb")) * 2 + lax.axis_index("zc")) * 2
    z = z + lax.axis_index("zd")
    lane = lax.axis_index("xl") * 2 + lax.axis_index("c")
    return lane, lax.axis_index("xh"), lax.axis_index("y"), z * 4 + lane


def home_of(index):
    turn = index & 15
    step = (turn >= 5).astype(jnp.int32) + (turn >= 11).astype(jnp.int32)
    first = 96 * turn - B * step
    start = jnp.where(turn == 11, 0, jnp.clip(first, 0, B - WIN))
    return 3 * (index >> 4) + step, first, start


def pack_kernel(owner_ref, pieces_ref, out_ref, count_ref):
    lane, xh, _, _ = where_am_i()
    for z in range(NZ):
        count_ref[z] = 0
        out_ref[z, :PIECE, :] = jnp.zeros((PIECE, 128), bf16)
        row, _, _ = home_of(z * 4 + lane)
        out_ref[z, PIECE:, :] = pieces_ref[xh * BROWS + row]

    for b in range(NBLK):
        who = owner_ref[b]
        z = who >> 2
        mine = (who & 3) == lane
        rank = count_ref[z]

        @pl.when(mine)
        def _():
            count_ref[z] = rank + 1

            @pl.when(rank == xh)
            def _():
                out_ref[z, :PIECE, :] = pieces_ref[(b % 2) * BROWS + b // 2]


def pack(owner, pieces):
    return pl.pallas_call(
        pack_kernel,
        out_shape=jax.ShapeDtypeStruct((NZ, 2 * PIECE, 128), bf16),
        in_specs=[
            pl.BlockSpec(memory_space=pltpu.SMEM),
            pl.BlockSpec(memory_space=pltpu.VMEM),
        ],
        out_specs=pl.BlockSpec(memory_space=pltpu.VMEM),
        scratch_shapes=[pltpu.SMEM((NZ,), jnp.int32)],
        name="pack",
    )(owner, pieces)


def root_rows(stat, parts, x_ref, c_ref):
    scale = 2.5 * lax.rsqrt(jnp.sum(stat * stat, keepdims=True) + 1e-06)
    current = scale * stat
    row = lax.broadcasted_iota(jnp.int32, (B, B), 0)
    col = lax.broadcasted_iota(jnp.int32, (B, B), 1)
    factor = (jnp.where(row == col, 1.25, 0.0) - 0.25 * current).astype(bf16)
    x_ref[...] = factor
    c_ref[...] = current.astype(bf16)
    root = (jnp.sqrt(jnp.sqrt(scale)) * factor.astype(f32)).astype(bf16)

    def dot(left, right):
        return jnp.dot(left, right, preferred_element_type=f32)

    rows = jnp.concatenate([x_ref[pl.ds(start, size), :] for start, size in parts], axis=0)
    eye = jnp.concatenate(
        [
            jnp.where(
                lax.broadcasted_iota(jnp.int32, (size, B), 0) + start
                == lax.broadcasted_iota(jnp.int32, (size, B), 1),
                1.25,
                0.0,
            )
            for start, size in parts
        ],
        axis=0,
    )
    square = dot(rows, factor).astype(bf16)
    fourth = dot(dot(square, factor).astype(bf16), factor).astype(bf16)
    second = (eye - 0.25 * dot(fourth, c_ref[...])).astype(bf16)
    return dot(second, root).astype(bf16)


def block_of(got_ref, which):
    return jnp.concatenate([got_ref[y, which] for y in range(NY)], axis=1)


def owned_kernel(owner_ref, got_ref, keep_ref, give_ref, xl_ref, cl_ref, xr_ref, cr_ref):
    _, xh, y, index = where_am_i()
    count = jnp.int32(0)
    for b in range(NBLK):
        count = count + (owner_ref[b] == index).astype(jnp.int32)
    block = block_of(got_ref, 0)
    left = lax.dot_general(block, block, NT, preferred_element_type=f32)
    right = lax.dot_general(block, block, TN, preferred_element_type=f32)
    share = B // 8
    first = pl.multiple_of(y * share + xh * (B // 2), share)
    second = pl.multiple_of(y * share + (1 - xh) * (B // 2), share)
    parts = ((first, share), (second, share))
    keep = (count > xh).astype(f32)
    for side, (stat, x_ref, c_ref) in enumerate(((left, xl_ref, cl_ref), (right, xr_ref, cr_ref))):
        rows = (root_rows(stat, parts, x_ref, c_ref).astype(f32) * keep).astype(bf16)
        keep_ref[side] = rows[:share]
        give_ref[side] = rows[share:]


def home_kernel(got_ref, out_ref, xl_ref, cl_ref, xr_ref, cr_ref):
    _, _, y, index = where_am_i()
    _, _, start = home_of(index)
    block = block_of(got_ref, 1)
    left = lax.dot_general(block, block, NT, preferred_element_type=f32)
    right = lax.dot_general(block, block, TN, preferred_element_type=f32)
    hr = root_rows(right, ((pl.multiple_of(y * 128, 128), 128),), xr_ref, cr_ref)
    hl = root_rows(left, ((pl.multiple_of(start, 32), WIN),), xl_ref, cl_ref)
    mixed = lax.dot_general(block, hr, NT, preferred_element_type=f32).astype(bf16)
    out_ref[...] = jnp.dot(hl, mixed, preferred_element_type=f32).astype(bf16)


def block_call(kernel, out_shapes, args, name):
    return pl.pallas_call(
        kernel,
        out_shape=[jax.ShapeDtypeStruct(shape, bf16) for shape in out_shapes],
        in_specs=[pl.BlockSpec(memory_space=pltpu.SMEM)] * (len(args) - 1)
        + [pl.BlockSpec(memory_space=pltpu.VMEM)],
        out_specs=[pl.BlockSpec(memory_space=pltpu.VMEM)] * len(out_shapes),
        scratch_shapes=[pltpu.VMEM((B, B), bf16)] * 4,
        compiler_params=pltpu.CompilerParams(vmem_limit_bytes=32 * 1024 * 1024),
        name=name,
    )(*args)


def add_up(got):
    return jnp.sum(got.astype(f32), axis=0).astype(bf16)


def per_device(inputs, cotangent, owner, step):
    xh, c = lax.axis_index("xh"), lax.axis_index("c")
    _, _, _, index = where_am_i()
    swap = [(0, 1), (1, 0)]
    half = inputs.shape[1] // 2

    def partial_grad(which):
        part = lax.dynamic_slice_in_dim(inputs, which * half, half, 1)
        return lax.dot_general(part, cotangent, TN, preferred_element_type=f32).astype(bf16)

    theirs = lax.ppermute(partial_grad(1 - c), "c", swap)
    ours = lax.optimization_barrier(partial_grad(c))
    grad = (ours.astype(f32) + theirs.astype(f32)).astype(bf16)
    grad = grad.reshape(2, LANE_BLOCKS, NZ // 2, 2, PIECE, 128).transpose(0, 3, 2, 1, 4, 5)
    got = all_to_all(grad.reshape(4, NZ // 2, LANE_BLOCKS * PIECE, 128), ("xl", "zd"))
    piece = add_up(all_to_all(add_up(got), ("za", "zb", "zc")))
    copies = jnp.broadcast_to(piece[None], (8,) + piece.shape)
    pieces = all_to_all(copies, ("xh", "c", "xl")).reshape(NBLK, PIECE, 128)
    got = all_to_all(pack(owner, pieces), ("za", "zb", "zc", "zd"))
    both = got.reshape(NZ, 2, PIECE, 128).transpose(1, 0, 2, 3).reshape(2, B, 128)
    got = all_to_all(jnp.broadcast_to(both[None], (NY, 2, B, 128)), "y")

    share = B // 8
    half = (2, share, B)
    keep, give = block_call(owned_kernel, (half, half), (owner, got), "owned")
    received = lax.ppermute(give, "xh", swap)
    (window,) = block_call(home_kernel, ((WIN, 128),), (got,), "home")
    _, first, start = home_of(index)
    turn = index & 15
    spare = jnp.where(turn == 4, window[WIN - 32 :], window[:32])
    extra = lax.ppermute(spare, "c", swap)
    roots = jnp.where(xh == 0, jnp.stack([keep, received]), jnp.stack([received, keep]))[None]

    whole = jnp.concatenate([extra, window, extra], axis=0)
    offset = jnp.where(turn == 5, 0, jnp.where(turn == 10, 96, 32 + first - start))
    mine = lax.dynamic_slice_in_dim(whole, offset, 96, 0)
    rate = peak_rate * jnp.minimum(1.0, (step[0].astype(f32) + 1.0) / warm_steps)
    update = (-rate * mine.astype(f32)).astype(bf16)
    return (update, roots)


def solution(mesh):
    names = ("xh", "y", "za", "zb", "zc", "zd", "xl", "c")
    split = Mesh(mesh.devices.reshape(2, NY, 2, 2, 2, 2, 2, 2), names)
    dp, role = names[2:], names[:2]
    return jax.shard_map(
        per_device,
        mesh=split,
        in_specs=(
            P(dp, None),
            P(dp, role),
            P(),
            P(),
        ),
        out_specs=(
            P(dp, role),
            P(dp, None, None, role, None),
        ),
        check_vma=False,
    )
```

```python
import jax
import jax.numpy as jnp
from jax import lax
from jax.experimental import pallas as pl
from jax.experimental.pallas import tpu as pltpu
from jax.sharding import Mesh, PartitionSpec as P

B = 512
peak_rate = 20.0
warm_steps = 64.0
bf16 = jnp.bfloat16
f32 = jnp.float32

NZ, NY = 16, 4
NBLK, BROWS = 24, 12
PIECE = B // NZ
LANE_BLOCKS = 3
LANE, XH, Y, START, VALID = range(NBLK, NBLK + 5)
WIN = 128

NT = (((1,), (1,)), ((), ()))
TN = (((0,), (0,)), ((), ()))


def all_to_all(value, axis):
    return lax.all_to_all(value, axis, 0, 0, tiled=True)


def small_call(kernel, out_shape, scalars, arrays, name, scratch=()):
    return pl.pallas_call(
        kernel,
        out_shape=jax.ShapeDtypeStruct(out_shape, bf16),
        in_specs=[pl.BlockSpec(memory_space=pltpu.SMEM)] * len(scalars)
        + [pl.BlockSpec(memory_space=pltpu.VMEM)] * len(arrays),
        out_specs=pl.BlockSpec(memory_space=pltpu.VMEM),
        scratch_shapes=list(scratch),
        compiler_params=pltpu.CompilerParams(vmem_limit_bytes=4 * 1024 * 1024),
        name=name,
    )(*scalars, *arrays)


def merge_kernel(ours_ref, theirs_ref, out_ref):
    for lo in range(2):
        for k in range(LANE_BLOCKS):
            for z in range(NZ):
                rows = pl.ds(((lo * LANE_BLOCKS + k) * NZ + z) * PIECE, PIECE)
                total = ours_ref[rows, :].astype(f32) + theirs_ref[rows, :].astype(f32)
                out_ref[lo * 2 + z % 2, z // 2, pl.ds(k * PIECE, PIECE), :] = total.astype(bf16)


def pack_kernel(place_ref, pieces_ref, out_ref, count_ref):
    lane, xh = place_ref[LANE], place_ref[XH]
    for z in range(NZ):
        count_ref[z] = 0
        out_ref[z, :PIECE, :] = jnp.zeros((PIECE, 128), bf16)
        turn = (z % 4) * 4 + lane
        row = 3 * (z // 4) + (turn >= 5).astype(jnp.int32) + (turn >= 11).astype(jnp.int32)
        out_ref[z, PIECE:, :] = pieces_ref[xh * BROWS + row]

    for b in range(NBLK):
        who = place_ref[b]
        z = who >> 2
        rank = count_ref[z]

        @pl.when((who & 3) == lane)
        def _():
            count_ref[z] = rank + 1

            @pl.when(rank == xh)
            def _():
                out_ref[z, :PIECE, :] = pieces_ref[(b % 2) * BROWS + b // 2]


def spread_kernel(got_ref, out_ref):
    for z in range(NZ):
        for which in range(2):
            rows = got_ref[z, which * PIECE : (which + 1) * PIECE, :]
            for y in range(NY):
                out_ref[y, which, z * PIECE : (z + 1) * PIECE, :] = rows


def root_rows(stat, parts, x_ref, c_ref):
    scale = 2.5 * lax.rsqrt(jnp.sum(stat * stat, keepdims=True) + 1e-06)
    current = scale * stat
    row = lax.broadcasted_iota(jnp.int32, (B, B), 0)
    col = lax.broadcasted_iota(jnp.int32, (B, B), 1)
    factor = (jnp.where(row == col, 1.25, 0.0) - 0.25 * current).astype(bf16)
    x_ref[...] = factor
    c_ref[...] = current.astype(bf16)
    root = (jnp.sqrt(jnp.sqrt(scale)) * factor.astype(f32)).astype(bf16)

    def dot(left, right):
        return jnp.dot(left, right, preferred_element_type=f32)

    rows = jnp.concatenate([x_ref[pl.ds(start, size), :] for start, size in parts], axis=0)
    eye = jnp.concatenate(
        [
            jnp.where(
                lax.broadcasted_iota(jnp.int32, (size, B), 0) + start
                == lax.broadcasted_iota(jnp.int32, (size, B), 1),
                1.25,
                0.0,
            )
            for start, size in parts
        ],
        axis=0,
    )
    square = dot(rows, factor).astype(bf16)
    fourth = dot(dot(square, factor).astype(bf16), factor).astype(bf16)
    second = (eye - 0.25 * dot(fourth, c_ref[...])).astype(bf16)
    return dot(second, root).astype(bf16)


def block_of(got_ref, which):
    return jnp.concatenate([got_ref[y, which] for y in range(NY)], axis=1)


def owned_kernel(place_ref, got_ref, keep_ref, give_ref, xl_ref, cl_ref, xr_ref, cr_ref):
    xh, y = place_ref[XH], place_ref[Y]
    block = block_of(got_ref, 0)
    left = lax.dot_general(block, block, NT, preferred_element_type=f32)
    right = lax.dot_general(block, block, TN, preferred_element_type=f32)
    share = B // 8
    first = pl.multiple_of(y * share + xh * (B // 2), share)
    second = pl.multiple_of(y * share + (1 - xh) * (B // 2), share)
    parts = ((first, share), (second, share))
    keep = place_ref[VALID].astype(f32)
    for side, (stat, x_ref, c_ref) in enumerate(((left, xl_ref, cl_ref), (right, xr_ref, cr_ref))):
        rows = (root_rows(stat, parts, x_ref, c_ref).astype(f32) * keep).astype(bf16)
        keep_ref[side] = rows[:share]
        give_ref[side] = rows[share:]


def home_kernel(place_ref, got_ref, out_ref, xl_ref, cl_ref, xr_ref, cr_ref):
    y, start = place_ref[Y], place_ref[START]
    block = block_of(got_ref, 1)
    left = lax.dot_general(block, block, NT, preferred_element_type=f32)
    right = lax.dot_general(block, block, TN, preferred_element_type=f32)
    hr = root_rows(right, ((pl.multiple_of(y * 128, 128), 128),), xr_ref, cr_ref)
    hl = root_rows(left, ((pl.multiple_of(start, 32), WIN),), xl_ref, cl_ref)
    mixed = lax.dot_general(block, hr, NT, preferred_element_type=f32).astype(bf16)
    out_ref[...] = jnp.dot(hl, mixed, preferred_element_type=f32).astype(bf16)


def block_call(kernel, out_shapes, place, got, name):
    return pl.pallas_call(
        kernel,
        out_shape=[jax.ShapeDtypeStruct(shape, bf16) for shape in out_shapes],
        in_specs=[
            pl.BlockSpec(memory_space=pltpu.SMEM),
            pl.BlockSpec(memory_space=pltpu.VMEM),
        ],
        out_specs=[pl.BlockSpec(memory_space=pltpu.VMEM)] * len(out_shapes),
        scratch_shapes=[pltpu.VMEM((B, B), bf16)] * 4,
        compiler_params=pltpu.CompilerParams(vmem_limit_bytes=16 * 1024 * 1024),
        name=name,
    )(place, got)


def add_up(got):
    total = got[0].astype(f32)
    for part in range(1, got.shape[0]):
        total = total + got[part].astype(f32)
    return total.astype(bf16)


def per_device(inputs, cotangent, owner, step):
    xh, y, c = lax.axis_index("xh"), lax.axis_index("y"), lax.axis_index("c")
    lane = lax.axis_index("xl") * 2 + c
    index = lax.axis_index(("za", "zb", "zc", "zd")) * 4 + lane
    swap = [(0, 1), (1, 0)]
    half = inputs.shape[1] // 2

    turn = index & 15
    first = 96 * turn - jnp.where(turn >= 11, 2 * B, jnp.where(turn >= 5, B, 0))
    start = jnp.where(turn == 11, 0, jnp.clip(first, 0, B - WIN))
    valid = (jnp.sum((owner == index).astype(jnp.int32)) > xh).astype(jnp.int32)
    place = jnp.concatenate([owner, jnp.stack([lane, xh, y, start, valid]).astype(jnp.int32)])
    cotangent, place = lax.optimization_barrier((cotangent.astype(f32), place))

    def partial_grad(which):
        part = lax.dynamic_slice_in_dim(inputs, which * half, half, 1)
        held = cotangent.astype(bf16)
        return lax.dot_general(part, held, TN, preferred_element_type=f32).astype(bf16)

    theirs = lax.ppermute(partial_grad(1 - c), "c", swap)
    ours = lax.optimization_barrier(partial_grad(c))
    shape = (4, NZ // 2, LANE_BLOCKS * PIECE, 128)
    got = all_to_all(small_call(merge_kernel, shape, (), (ours, theirs), "merge"), ("xl", "zd"))
    piece = add_up(all_to_all(add_up(got), ("za", "zb", "zc")))
    copies = jnp.broadcast_to(piece[None], (8,) + piece.shape)
    pieces = all_to_all(copies, ("xh", "c", "xl")).reshape(NBLK, PIECE, 128)
    shape = (NZ, 2 * PIECE, 128)
    count = pltpu.SMEM((NZ,), jnp.int32)
    sent = small_call(pack_kernel, shape, (place,), (pieces,), "pack", (count,))
    got = all_to_all(sent, ("za", "zb", "zc", "zd"))
    got = all_to_all(small_call(spread_kernel, (NY, 2, B, 128), (), (got,), "spread"), "y")

    share = B // 8
    half = (2, share, B)
    keep, give = block_call(owned_kernel, (half, half), place, got, "owned")
    received = lax.ppermute(give, "xh", swap)
    (window,) = block_call(home_kernel, ((WIN, 128),), place, got, "home")
    spare = jnp.where(turn == 4, window[WIN - 32 :], window[:32])
    extra = lax.ppermute(spare, "c", swap)
    roots = jnp.where(xh == 0, jnp.stack([keep, received]), jnp.stack([received, keep]))[None]

    whole = jnp.concatenate([extra, window, extra], axis=0)
    offset = jnp.where(turn == 5, 0, jnp.where(turn == 10, 96, 32 + first - start))
    mine = lax.dynamic_slice_in_dim(whole, offset, 96, 0)
    rate = peak_rate * jnp.minimum(1.0, (step[0].astype(f32) + 1.0) / warm_steps)
    update = (-rate * mine.astype(f32)).astype(bf16)
    return (update, roots)


def solution(mesh):
    names = ("xh", "y", "za", "zb", "zc", "zd", "xl", "c")
    split = Mesh(mesh.devices.reshape(2, NY, 2, 2, 2, 2, 2, 2), names)
    dp, role = names[2:], names[:2]
    return jax.shard_map(
        per_device,
        mesh=split,
        in_specs=(
            P(dp, None),
            P(dp, role),
            P(),
            P(),
        ),
        out_specs=(
            P(dp, role),
            P(dp, None, None, role, None),
        ),
        check_vma=False,
    )
```
